512 devices in a mesh: layer: 32 (over z, x), panel: 16 (over y, core).
Axes of the slice: x: 4, y: 8, z: 8, core: 2. Of those that a mesh axis runs over, the one named last changes fastest.
Arguments:
- lower_blocks: bfloat16 [32, 512, 512], P('layer', 'panel'), may hold values from -2 to 0.5
- diag_blocks: bfloat16 [32, 512, 512], P('layer', 'panel'), may hold values from -0.5 to 4, as said below
- upper_blocks: bfloat16 [32, 512, 512], P('layer', 'panel'), may hold values from -2 to 0.5
- right_sides: bfloat16 [32, 512, 128], P('layer', 'panel'), may hold values from -6 to 6
Outputs:
- reduced_diag: bfloat16 [32, 512, 512], P('layer', 'panel')
- reduced_rhs: bfloat16 [32, 512, 128], P('layer', 'panel')
The draws below stay inside these ranges and needn't reach their ends.
Inputs may be any that keep to these rules, and one draw needn't show every extreme that they name: `diag_blocks`: the diagonal entries of every diagonal block lie between 2 and 4.
All inputs are finite; a program needn't handle non-finite values.
Results may differ from the reference program's by a relative error of at most 0.035.
Values may be sent and summed in bfloat16 or wider, within the bound.
No kernel may reach another device: no remote copies, remote signals or barrier semaphores. Data moves between devices by JAX's collectives and lax.ppermute only.
A program may use at most 64 MiB of HBM per device.

```python
import jax
import jax.numpy as jnp
from jax import lax

M = 512
R = 128
LEVELS = 3
LAYERS = 32


def diagonal_values(key):
    return jnp.exp(jax.random.uniform(jax.random.fold_in(key, 7), (LAYERS, M), jnp.float32, jnp.log(2.0), jnp.log(4.0)))


def coupling_draw(key, salt, toward):
    key_noise = jax.random.fold_in(jax.random.fold_in(key, salt), 0)
    key_ratio = jax.random.fold_in(jax.random.fold_in(key, salt), 2)
    values = diagonal_values(key)
    if toward < 0:
        neighbour = jnp.concatenate([values[:1], values[:-1]], axis=0)
    else:
        neighbour = jnp.concatenate([values[1:], values[-1:]], axis=0)
    coupling_ratio = jax.random.uniform(key_ratio, (LAYERS, M), jnp.float32, 0.41, 0.48)
    strength = -coupling_ratio * jnp.sqrt(values * neighbour)
    noise = jax.random.truncated_normal(key_noise, -4.0, 4.0, (LAYERS, M, M), jnp.float32)
    identity = jnp.eye(M, dtype=jnp.float32)
    block = noise * (0.45 / jnp.sqrt(M * 1.0)) * (1.0 - identity) + identity * strength[:, :, None]
    return block.astype(jnp.bfloat16)


def draw_lower_blocks(key, part):
    return coupling_draw(key, 21, -1)


def draw_upper_blocks(key, part):
    return coupling_draw(key, 31, 1)


def draw_diag_blocks(key, part):
    key_noise = jax.random.fold_in(jax.random.fold_in(key, 11), 0)
    diag_values = diagonal_values(key)
    noise = jax.random.truncated_normal(key_noise, -4.0, 4.0, (LAYERS, M, M), jnp.float32)
    identity = jnp.eye(M, dtype=jnp.float32)
    block = noise * (0.65 / jnp.sqrt(M * 1.0)) * (1.0 - identity) + identity * diag_values[:, :, None]
    return block.astype(jnp.bfloat16)


def levels(own_key, extent, cuts, low, high):
    factor_of, own = 1.0, jax.random.fold_in(own_key, 6)
    for position, blocks in cuts:
        draws = jnp.exp(jax.random.uniform(jax.random.fold_in(own, position), (blocks,), jnp.float32, low / len(cuts), high / len(cuts)))
        factor_of = factor_of * jnp.repeat(draws, extent[position] // blocks).reshape([-1 if axis == position else 1 for axis in range(len(extent))])
    return factor_of


def centred(own_key, extent, scale, most, cuts=(), kind=jnp.bfloat16):
    result = scale * jax.random.normal(own_key, extent, jnp.float32)
    if cuts:
        result = result * levels(own_key, extent, cuts, -0.22, 0.18)
    return jnp.clip(result, -most, most).astype(kind)


def setup_inputs(seed: int = 0) -> dict:
    arg_keys = jax.random.split(jax.random.key(seed), 5)
    return {
        "lower_blocks": draw_lower_blocks(jax.random.fold_in(arg_keys[4], 71), 0),
        "diag_blocks": draw_diag_blocks(jax.random.fold_in(arg_keys[4], 71), 0),
        "upper_blocks": draw_upper_blocks(jax.random.fold_in(arg_keys[4], 71), 0),
        "right_sides": centred(arg_keys[3], (LAYERS, M, R), 1.0, 6.0, ((0, 32), (1, 16))),
    }


def start_inverse(diag_block):
    inverse_diag = 1.0 / jnp.diagonal(diag_block).astype(jnp.float32)
    identity = jnp.eye(diag_block.shape[0], dtype=jnp.float32)
    guess = 2.0 * identity * inverse_diag[:, None] - inverse_diag[:, None] * diag_block.astype(jnp.float32) * inverse_diag[None, :]
    return guess.astype(jnp.bfloat16)


def invert(diag_block):
    first_guess = start_inverse(diag_block)
    product = jnp.dot(first_guess, diag_block, preferred_element_type=jnp.float32).astype(jnp.bfloat16)
    second = 2.0 * first_guess.astype(jnp.float32) - jnp.dot(product, first_guess, preferred_element_type=jnp.float32)
    return second.astype(jnp.bfloat16)


def solve_products(operands):
    diag_block, stacked = operands
    return jnp.dot(invert(diag_block), stacked, preferred_element_type=jnp.float32).astype(jnp.bfloat16)


def couple(operands):
    left_side, right_side = operands
    return jnp.dot(left_side, right_side, preferred_element_type=jnp.float32)


def eliminate(lower_rows, diag_rows, upper_rows, rhs_rows, terms_left, terms_right, order_size):
    new_lower = (-terms_left[..., :order_size]).astype(jnp.bfloat16)
    new_diag = (diag_rows.astype(jnp.float32) - terms_left[..., order_size:2 * order_size] - terms_right[..., :order_size]).astype(jnp.bfloat16)
    new_upper = (-terms_right[..., order_size:2 * order_size]).astype(jnp.bfloat16)
    new_rhs = (rhs_rows.astype(jnp.float32) - terms_left[..., 2 * order_size:] - terms_right[..., 2 * order_size:]).astype(jnp.bfloat16)
    return new_lower, new_diag, new_upper, new_rhs


def reference(lower_blocks, diag_blocks, upper_blocks, right_sides):
    order_size = lower_blocks.shape[1]
    for level_index in range(LEVELS):
        reach = 2 ** level_index
        stacked = jnp.concatenate([lower_blocks, upper_blocks, right_sides], axis=2)
        products = lax.map(solve_products, (diag_blocks, stacked))
        padding = jnp.zeros((reach,) + products.shape[1:], jnp.bfloat16)
        preceding = jnp.concatenate([padding, products[:-reach]], axis=0)
        following = jnp.concatenate([products[reach:], padding], axis=0)
        terms_left = lax.map(couple, (lower_blocks, preceding))
        terms_right = lax.map(couple, (upper_blocks, following))
        lower_blocks, diag_blocks, upper_blocks, right_sides = eliminate(lower_blocks, diag_blocks, upper_blocks, right_sides, terms_left, terms_right, order_size)
    return diag_blocks, right_sides
```

```python
import jax
import jax.numpy as jnp
from jax import lax
from jax.experimental import pallas as pl
from jax.experimental.pallas import tpu as pltpu
from jax.sharding import Mesh
from jax.sharding import PartitionSpec as P

LAYERS = 32
AXES = ("layer", "chip", "c")


def send(block, by):
    pairs = [(i, i + by) for i in range(LAYERS) if 0 <= i + by < LAYERS]
    return lax.ppermute(block, "layer", pairs)


def swap(block):
    return lax.ppermute(block, "c", [(0, 1), (1, 0)])


def dot(a, b):
    return jnp.dot(a, b, preferred_element_type=jnp.float32)


def dot_across(a, b):
    return lax.dot_general(a, b, (((1,), (1,)), ((), ())), preferred_element_type=jnp.float32)


def half_of(block, core):
    h = block.shape[1] // 2
    return jnp.where(core == 0, block[:, :h], block[:, h:])


def inverse(diag):
    order = diag.shape[0]
    eye = jnp.eye(order, dtype=jnp.bool_)
    wide = diag.astype(jnp.float32)
    picked = jnp.where(eye, wide, 0.0)
    across = 1.0 / jnp.sum(picked, axis=0, keepdims=True)
    down = 1.0 / jnp.sum(picked, axis=1, keepdims=True)
    guess = jnp.where(eye, 2.0 * down, 0.0) - down * wide * across
    guess = guess.astype(jnp.bfloat16)
    product = dot(guess, diag).astype(jnp.bfloat16)
    return (2.0 * guess.astype(jnp.float32) - dot(product, guess)).astype(jnp.bfloat16)


def after(diag, rhs, left, right):
    h, f = diag.shape[1], rhs.shape[1]
    new_diag = diag.astype(jnp.float32) - left[:, h + f :] - right[:, :h]
    new_rhs = rhs.astype(jnp.float32) - left[:, h : h + f] - right[:, h : h + f]
    mine = jnp.concatenate([new_diag, -left[:, :h], -right[:, h + f :]], axis=1)
    return mine.astype(jnp.bfloat16), new_rhs.astype(jnp.bfloat16)


def solve_kernel(core_ref, mine_ref, other_ref, rhs_ref, solved_ref, lower_ref, upper_ref, diag_ref):
    h = diag_ref.shape[1] // 2
    f = rhs_ref.shape[1]
    for own in range(2):

        @pl.when(core_ref[0] == own)
        def _(own=own):
            low, high = (mine_ref, other_ref) if own == 0 else (other_ref, mine_ref)
            for k, whole in enumerate((diag_ref, lower_ref, upper_ref)):
                whole[:, :h] = low[:, k * h : (k + 1) * h]
                whole[:, h:] = high[:, k * h : (k + 1) * h]

    found = inverse(diag_ref[...])

    def solved(right):
        return dot(found, right).T.astype(jnp.bfloat16)

    solved_ref[:h] = solved(mine_ref[:, h : 2 * h])
    solved_ref[h : h + f] = solved(rhs_ref[...])
    solved_ref[h + f :] = solved(mine_ref[:, 2 * h :])


def solve(mine, rhs, core):
    m, f = rhs.shape
    h = m // 2
    square = jax.ShapeDtypeStruct((m, m), jnp.bfloat16)
    whole = pl.BlockSpec(memory_space=pltpu.VMEM)
    return pl.pallas_call(
        solve_kernel,
        out_shape=(jax.ShapeDtypeStruct((m + f, m), jnp.bfloat16), square, square),
        in_specs=[pl.BlockSpec(memory_space=pltpu.SMEM), whole, whole, whole],
        out_specs=(whole, whole, whole),
        scratch_shapes=[pltpu.VMEM((m, m), jnp.bfloat16)],
        compiler_params=pltpu.CompilerParams(vmem_limit_bytes=24 * 2**20),
        cost_estimate=pl.CostEstimate(flops=2 * m * m * (3 * m + f), bytes_accessed=12 * m * m, transcendentals=0),
    )(core.reshape(1).astype(jnp.int32), mine, swap(mine), rhs)


def whole_layer(rows, core):
    copies = jnp.broadcast_to(rows[None], (8, *rows.shape))
    mine = lax.all_to_all(copies, "chip", 0, 0, tiled=True)
    other = swap(mine)
    both = jnp.stack([jnp.where(core == 0, mine, other), jnp.where(core == 0, other, mine)], axis=1)
    return both.reshape(-1, rows.shape[1])


def on_device(lower_blocks, diag_blocks, upper_blocks, right_sides):
    core = lax.axis_index("c")
    m, r = lower_blocks.shape[2], right_sides.shape[2]
    h, f = m // 2, r // 2
    own = (diag_blocks[0], lower_blocks[0], upper_blocks[0], right_sides[0])
    full = whole_layer(jnp.concatenate(own, axis=1), core)
    diag, lower, upper, rhs = full[:, :m], full[:, m : 2 * m], full[:, 2 * m : 3 * m], full[:, 3 * m :]
    wide = jnp.concatenate([half_of(lower, core), half_of(rhs, core), half_of(upper, core)], axis=1)
    solved = dot(inverse(diag), wide).astype(jnp.bfloat16)
    left = dot(lower, send(solved, 1))
    right = dot(upper, send(solved, -1))
    mine, rhs = after(half_of(diag, core), half_of(rhs, core), left, right)
    solved, lower, upper = solve(mine, rhs, core)
    left = dot_across(lower, send(solved, 2))
    right = dot_across(upper, send(solved, -2))
    mine, rhs = after(mine[:, :h], rhs, left, right)
    solved, lower, upper = solve(mine, rhs, core)
    forward = send(solved[h:], 4)
    back = send(solved[: h + f], -4)
    n = 2 * own[0].shape[0]
    at = lax.axis_index("chip") * n

    def rows_of(block):
        return lax.dynamic_slice_in_dim(block, at, n, axis=0)

    left = dot_across(rows_of(lower), forward)
    right = dot_across(rows_of(upper), back)
    new_diag = rows_of(mine[:, :h]).astype(jnp.float32) - left[:, f:] - right[:, :h]
    new_rhs = rows_of(rhs).astype(jnp.float32) - left[:, :f] - right[:, h:]
    done = jnp.concatenate([new_diag, new_rhs], axis=1).astype(jnp.bfloat16)
    done = lax.all_gather(done, "c", axis=0)
    mine = jnp.where(core == 0, done[:, : n // 2], done[:, n // 2 :])
    out_diag = jnp.concatenate([mine[0, :, :h], mine[1, :, :h]], axis=1)
    out_rhs = jnp.concatenate([mine[0, :, h:], mine[1, :, h:]], axis=1)
    return out_diag[None], out_rhs[None]


def solution(mesh):
    finer = Mesh(mesh.devices.reshape(LAYERS, 8, 2), AXES)
    placed = P("layer", ("chip", "c"), None)
    return jax.shard_map(
        on_device,
        mesh=finer,
        in_specs=(placed,) * 4,
        out_specs=(placed,) * 2,
        check_vma=False,
    )
```

```python
import jax
import jax.numpy as jnp
from jax import lax
from jax.experimental import pallas as pl
from jax.experimental.pallas import tpu as pltpu
from jax.sharding import Mesh
from jax.sharding import PartitionSpec as P

LAYERS = 32
AXES = ("layer", "far", "near", "c")


def send(block, by):
    pairs = [(i, i + by) for i in range(LAYERS) if 0 <= i + by < LAYERS]
    return lax.ppermute(block, "layer", pairs)


def swap(block):
    return lax.ppermute(block, "c", [(0, 1), (1, 0)])


def of_cores(rows):
    return lax.all_gather(rows, "c", axis=0, tiled=True)


def of_pair(rows):
    return lax.all_gather(rows, "near", axis=0, tiled=True)


def dot(a, b):
    return jnp.dot(a, b, preferred_element_type=jnp.float32)


def dot_across(a, b):
    return lax.dot_general(a, b, (((1,), (1,)), ((), ())), preferred_element_type=jnp.float32)


def inverse(diag):
    order = diag.shape[0]
    eye = jnp.eye(order, dtype=jnp.bool_)
    wide = diag.astype(jnp.float32)
    picked = jnp.where(eye, wide, 0.0)
    across = 1.0 / jnp.sum(picked, axis=0, keepdims=True)
    down = 1.0 / jnp.sum(picked, axis=1, keepdims=True)
    guess = jnp.where(eye, 2.0 * down, 0.0) - down * wide * across
    guess = guess.astype(jnp.bfloat16)
    product = dot(guess, diag).astype(jnp.bfloat16)
    return (2.0 * guess.astype(jnp.float32) - dot(product, guess)).astype(jnp.bfloat16)


def solve_kernel(diag_ref, *refs):
    solved_ref = refs[-1]
    found = inverse(diag_ref[...])
    at = 0
    for ref in refs[:-1]:
        rows = ref.shape[0]
        solved_ref[at : at + rows] = dot(ref[...], found).astype(jnp.bfloat16)
        at += rows


def solve(diag, parts):
    m = diag.shape[0]
    rows = sum(p.shape[0] for p in parts)
    whole = pl.BlockSpec(memory_space=pltpu.VMEM)
    return pl.pallas_call(
        solve_kernel,
        out_shape=jax.ShapeDtypeStruct((rows, m), jnp.bfloat16),
        in_specs=[whole] * (1 + len(parts)),
        out_specs=whole,
        compiler_params=pltpu.CompilerParams(vmem_limit_bytes=24 * 2**20),
        cost_estimate=pl.CostEstimate(flops=2 * m * m * (2 * m + rows), bytes_accessed=4 * m * (m + rows), transcendentals=0),
    )(diag, *parts)


def after(diag, rhs, left, right):
    h, f = diag.shape[0], rhs.shape[0]
    new_diag = diag.astype(jnp.float32) - left[h + f :] - right[:h]
    new_rhs = rhs.astype(jnp.float32) - left[h : h + f] - right[h : h + f]
    new = (new_diag, -left[:h], -right[h + f :], new_rhs)
    return tuple(a.astype(jnp.bfloat16) for a in new)


def first_kernel(core_ref, mine_ref, other_ref, solved_ref, lower_ref, upper_ref, diag_out, rhs_out, diag_ref, rhs_ref):
    m = diag_ref.shape[0]
    n = mine_ref.shape[1]
    wholes = ((diag_ref, 0, m), (lower_ref, m, m), (upper_ref, 2 * m, m), (rhs_ref, 3 * m, rhs_ref.shape[1]))
    for own in range(2):

        @pl.when(core_ref[0] == own)
        def _(own=own):
            for k in range(mine_ref.shape[0]):
                for ref, c in ((mine_ref, own), (other_ref, 1 - own)):
                    at = (2 * k + c) * n
                    for whole, left, width in wholes:
                        whole[at : at + n] = ref[k, :, left : left + width]

    found = inverse(diag_ref[...])
    q, g = solved_ref.shape[1] // 4, rhs_out.shape[0]
    for k in range(4):

        @pl.when(core_ref[1] == k)
        def _(k=k):
            side = slice(k * q, k * q + q)
            small = slice(k * g, k * g + g)

            def solved(right):
                return dot(found, right).T.astype(jnp.bfloat16)

            solved_ref[:q] = solved(lower_ref[:, side])
            solved_ref[q + g :] = solved(upper_ref[:, side])
            solved_ref[q : q + g] = solved(rhs_ref[:, small])
            diag_out[...] = diag_ref[:, side].T
            rhs_out[...] = rhs_ref[:, small].T


def first_solve(rows, core, quarter, m):
    copies = jnp.broadcast_to(rows[None], (8, *rows.shape))
    mine = lax.all_to_all(copies, ("far", "near"), 0, 0, tiled=True)
    r = rows.shape[1] - 3 * m
    whole = pl.BlockSpec(memory_space=pltpu.VMEM)
    shapes = (((2 * m + r) // 4, m), (m, m), (m, m), (m // 4, m), (r // 4, m))
    return pl.pallas_call(
        first_kernel,
        out_shape=tuple(jax.ShapeDtypeStruct(s, jnp.bfloat16) for s in shapes),
        in_specs=[pl.BlockSpec(memory_space=pltpu.SMEM), whole, whole],
        out_specs=(whole,) * 5,
        scratch_shapes=[pltpu.VMEM((m, m), jnp.bfloat16), pltpu.VMEM((m, r), jnp.bfloat16)],
        compiler_params=pltpu.CompilerParams(vmem_limit_bytes=24 * 2**20),
        cost_estimate=pl.CostEstimate(flops=7 * m * m * m, bytes_accessed=16 * m * m, transcendentals=0),
    )(jnp.stack([core, quarter]).astype(jnp.int32), mine, swap(mine))


def on_device(lower_blocks, diag_blocks, upper_blocks, right_sides):
    core, near = lax.axis_index("c"), lax.axis_index("near")
    m, r = lower_blocks.shape[2], right_sides.shape[2]
    q, g = m // 4, r // 4
    own = (diag_blocks[0], lower_blocks[0], upper_blocks[0], right_sides[0])
    rows = jnp.concatenate(own, axis=1)
    solved, lower, upper, diag, rhs = first_solve(rows, core, core * 2 + near, m)
    left, right = dot_across(send(solved, 1), lower), dot_across(send(solved, -1), upper)
    diag, lower, upper, rhs = after(diag, rhs, left, right)

    solved = solve(of_cores(of_pair(diag)), (lower, rhs, upper))
    solved, lower, upper = lax.optimization_barrier((solved, lower, upper))
    ahead, behind = send(solved, 2), send(solved, -2)
    both = lax.all_gather(jnp.concatenate([lower, upper], axis=0), "near", axis=0)
    lower = of_cores(jnp.concatenate([both[0, :q], both[1, :q]], axis=0))
    upper = of_cores(jnp.concatenate([both[0, q:], both[1, q:]], axis=0))
    diag, lower, upper, rhs = after(diag, rhs, dot(ahead, lower), dot(behind, upper))

    solved = solve(of_cores(of_pair(diag)), (lower, rhs, upper))
    solved, lower, upper = lax.optimization_barrier((solved, lower, upper))
    forward, back = send(solved[q:], 4), send(solved[: q + g], -4)
    n = own[0].shape[0]
    at = lax.axis_index("far") * (4 * n)

    def rows_of(block):
        return lax.dynamic_slice_in_dim(block, at, 4 * n, axis=1)

    couplings = of_cores(of_pair(jnp.concatenate([rows_of(lower), rows_of(upper)], axis=1)))
    left = dot(forward, couplings[:, : 4 * n])
    right = dot(back, couplings[:, 4 * n :])
    new_diag = rows_of(diag).astype(jnp.float32) - left[g:] - right[:q]
    new_rhs = rows_of(rhs).astype(jnp.float32) - left[:g] - right[q:]
    done = jnp.concatenate([new_diag, new_rhs], axis=0).astype(jnp.bfloat16)
    done = lax.all_gather(done, "near", axis=0)
    done = jnp.where(near == 0, done[:, :, : 2 * n], done[:, :, 2 * n :])
    done = lax.all_gather(done, "c", axis=0)
    done = jnp.where(core == 0, done[..., :n], done[..., n:])
    out_diag = done[:, :, :q].reshape(m, n).T
    out_rhs = done[:, :, q:].reshape(r, n).T
    return out_diag[None], out_rhs[None]


def solution(mesh):
    finer = Mesh(mesh.devices.reshape(LAYERS, 4, 2, 2), AXES)
    placed = P("layer", ("far", "near", "c"), None)
    return jax.shard_map(
        on_device,
        mesh=finer,
        in_specs=(placed,) * 4,
        out_specs=(placed,) * 2,
        check_vma=False,
    )
```

```python
import jax
import jax.numpy as jnp
from jax import lax
from jax.experimental import pallas as pl
from jax.experimental.pallas import tpu as pltpu
from jax.sharding import Mesh
from jax.sharding import PartitionSpec as P

LAYERS = 32
AXES = ("layer", "far", "near", "c")


def send(block, by):
    pairs = [(i, i + by) for i in range(LAYERS) if 0 <= i + by < LAYERS]
    return lax.ppermute(block, "layer", pairs)


def swap(block):
    return lax.ppermute(block, "c", [(0, 1), (1, 0)])


def of_cores(rows):
    return lax.all_gather(rows, "c", axis=0, tiled=True)


def of_pair(rows):
    return lax.all_gather(rows, "near", axis=0, tiled=True)


def dot(a, b):
    return jnp.dot(a, b, preferred_element_type=jnp.float32)


def dot_across(a, b):
    return lax.dot_general(a, b, (((1,), (1,)), ((), ())), preferred_element_type=jnp.float32)


def inverse(diag):
    order = diag.shape[0]
    eye = jnp.eye(order, dtype=jnp.bool_)
    wide = diag.astype(jnp.float32)
    picked = jnp.where(eye, wide, 0.0)
    across = 1.0 / jnp.sum(picked, axis=0, keepdims=True)
    down = 1.0 / jnp.sum(picked, axis=1, keepdims=True)
    guess = jnp.where(eye, 2.0 * down, 0.0) - down * wide * across
    guess = guess.astype(jnp.bfloat16)
    product = dot(guess, diag).astype(jnp.bfloat16)
    return (2.0 * guess.astype(jnp.float32) - dot(product, guess)).astype(jnp.bfloat16)


def solve_kernel(diag_ref, *refs):
    solved_ref = refs[-1]
    found = inverse(diag_ref[...])
    at = 0
    for ref in refs[:-1]:
        rows = ref.shape[0]
        solved_ref[at : at + rows] = dot(ref[...], found).astype(jnp.bfloat16)
        at += rows


def solve(diag, parts):
    m = diag.shape[0]
    rows = sum(p.shape[0] for p in parts)
    whole = pl.BlockSpec(memory_space=pltpu.VMEM)
    return pl.pallas_call(
        solve_kernel,
        out_shape=jax.ShapeDtypeStruct((rows, m), jnp.bfloat16),
        in_specs=[whole] * (1 + len(parts)),
        out_specs=whole,
        compiler_params=pltpu.CompilerParams(vmem_limit_bytes=24 * 2**20),
        cost_estimate=pl.CostEstimate(flops=2 * m * m * (2 * m + rows), bytes_accessed=4 * m * (m + rows), transcendentals=0),
    )(diag, *parts)


def finish_kernel(core_ref, done_ref, diag_ref, rhs_ref):
    n = diag_ref.shape[1]
    q, g = diag_ref.shape[2] // 4, rhs_ref.shape[2] // 4
    for own in range(2):

        @pl.when(core_ref[0] == own)
        def _(own=own):
            for k in range(4):
                turned = done_ref[k // 2, k % 2].astype(jnp.float32).T
                turned = turned[own * n : own * n + n].astype(jnp.bfloat16)
                diag_ref[0, :, k * q : k * q + q] = turned[:, :q]
                rhs_ref[0, :, k * g : k * g + g] = turned[:, q:]


def finish(done, core, n, m, r):
    whole = pl.BlockSpec(memory_space=pltpu.VMEM)
    shapes = ((1, n, m), (1, n, r))
    return pl.pallas_call(
        finish_kernel,
        out_shape=tuple(jax.ShapeDtypeStruct(s, jnp.bfloat16) for s in shapes),
        in_specs=[pl.BlockSpec(memory_space=pltpu.SMEM), whole],
        out_specs=(whole, whole),
        compiler_params=pltpu.CompilerParams(vmem_limit_bytes=8 * 2**20),
        cost_estimate=pl.CostEstimate(flops=m * n, bytes_accessed=4 * m * n, transcendentals=0),
    )(core.reshape(1).astype(jnp.int32), done)


def after(diag, rhs, left, right):
    h, f = diag.shape[0], rhs.shape[0]
    new_diag = diag.astype(jnp.float32) - left[h + f :] - right[:h]
    new_rhs = rhs.astype(jnp.float32) - left[h : h + f] - right[h : h + f]
    new = (new_diag, -left[:h], -right[h + f :], new_rhs)
    return tuple(a.astype(jnp.bfloat16) for a in new)


def first_kernel(core_ref, mine_ref, other_ref, solved_ref, lower_ref, upper_ref, diag_out, rhs_out, diag_ref, rhs_ref):
    m = diag_ref.shape[0]
    n = mine_ref.shape[1]
    wholes = ((diag_ref, 0, m), (lower_ref, m, m), (upper_ref, 2 * m, m), (rhs_ref, 3 * m, rhs_ref.shape[1]))
    for own in range(2):

        @pl.when(core_ref[0] == own)
        def _(own=own):
            for k in range(mine_ref.shape[0]):
                for ref, c in ((mine_ref, own), (other_ref, 1 - own)):
                    at = (2 * k + c) * n
                    for whole, left, width in wholes:
                        whole[at : at + n] = ref[k, :, left : left + width]

    found = inverse(diag_ref[...])
    q, g = solved_ref.shape[1] // 4, rhs_out.shape[0]
    for k in range(4):

        @pl.when(core_ref[1] == k)
        def _(k=k):
            side = slice(k * q, k * q + q)
            small = slice(k * g, k * g + g)

            def solved(right):
                return dot(found, right).T.astype(jnp.bfloat16)

            solved_ref[:q] = solved(lower_ref[:, side])
            solved_ref[q + g :] = solved(upper_ref[:, side])
            solved_ref[q : q + g] = solved(rhs_ref[:, small])
            diag_out[...] = diag_ref[:, side].T
            rhs_out[...] = rhs_ref[:, small].T


def first_solve(rows, core, quarter, m):
    copies = jnp.broadcast_to(rows[None], (8, *rows.shape))
    mine = lax.all_to_all(copies, ("far", "near"), 0, 0, tiled=True)
    r = rows.shape[1] - 3 * m
    whole = pl.BlockSpec(memory_space=pltpu.VMEM)
    shapes = (((2 * m + r) // 4, m), (m, m), (m, m), (m // 4, m), (r // 4, m))
    return pl.pallas_call(
        first_kernel,
        out_shape=tuple(jax.ShapeDtypeStruct(s, jnp.bfloat16) for s in shapes),
        in_specs=[pl.BlockSpec(memory_space=pltpu.SMEM), whole, whole],
        out_specs=(whole,) * 5,
        scratch_shapes=[pltpu.VMEM((m, m), jnp.bfloat16), pltpu.VMEM((m, r), jnp.bfloat16)],
        compiler_params=pltpu.CompilerParams(vmem_limit_bytes=24 * 2**20),
        cost_estimate=pl.CostEstimate(flops=7 * m * m * m, bytes_accessed=16 * m * m, transcendentals=0),
    )(jnp.stack([core, quarter]).astype(jnp.int32), mine, swap(mine))


def on_device(lower_blocks, diag_blocks, upper_blocks, right_sides):
    core, near = lax.axis_index("c"), lax.axis_index("near")
    m, r = lower_blocks.shape[2], right_sides.shape[2]
    q, g = m // 4, r // 4
    own = (diag_blocks[0], lower_blocks[0], upper_blocks[0], right_sides[0])
    rows = jnp.concatenate(own, axis=1)
    solved, lower, upper, diag, rhs = first_solve(rows, core, core * 2 + near, m)
    left, right = dot_across(send(solved, 1), lower), dot_across(send(solved, -1), upper)
    diag, lower, upper, rhs = after(diag, rhs, left, right)

    solved = solve(of_cores(of_pair(diag)), (lower, rhs, upper))
    solved, lower, upper = lax.optimization_barrier((solved, lower, upper))
    ahead, behind = send(solved, 2), send(solved, -2)
    both = lax.all_gather(jnp.concatenate([lower, upper], axis=0), "near", axis=0)
    lower = of_cores(jnp.concatenate([both[0, :q], both[1, :q]], axis=0))
    upper = of_cores(jnp.concatenate([both[0, q:], both[1, q:]], axis=0))
    diag, lower, upper, rhs = after(diag, rhs, dot(ahead, lower), dot(behind, upper))

    solved = solve(of_cores(of_pair(diag)), (lower, rhs, upper))
    solved, lower, upper = lax.optimization_barrier((solved, lower, upper))
    forward, back = send(solved[q:], 4), send(solved[: q + g], -4)
    n = own[0].shape[0]
    at = lax.axis_index("far") * (4 * n)

    def rows_of(block):
        return lax.dynamic_slice_in_dim(block, at, 4 * n, axis=1)

    couplings = of_cores(of_pair(jnp.concatenate([rows_of(lower), rows_of(upper)], axis=1)))
    left = dot(forward, couplings[:, : 4 * n])
    right = dot(back, couplings[:, 4 * n :])
    new_diag = rows_of(diag).astype(jnp.float32) - left[g:] - right[:q]
    new_rhs = rows_of(rhs).astype(jnp.float32) - left[:g] - right[q:]
    done = jnp.concatenate([new_diag, new_rhs], axis=0).astype(jnp.bfloat16)
    done = lax.all_gather(done, "near", axis=0)
    done = jnp.where(near == 0, done[:, :, : 2 * n], done[:, :, 2 * n :])
    done = lax.all_gather(done, "c", axis=0)
    return finish(done, core, n, m, r)


def solution(mesh):
    finer = Mesh(mesh.devices.reshape(LAYERS, 4, 2, 2), AXES)
    placed = P("layer", ("far", "near", "c"), None)
    return jax.shard_map(
        on_device,
        mesh=finer,
        in_specs=(placed,) * 4,
        out_specs=(placed,) * 2,
        check_vma=False,
    )
```

```python
import jax
import jax.numpy as jnp
from jax import lax
from jax.experimental import pallas as pl
from jax.experimental.pallas import tpu as pltpu
from jax.sharding import Mesh
from jax.sharding import PartitionSpec as P

LAYERS = 32
AXES = ("layer", "far", "near", "c")


def send(block, by):
    pairs = [(i, i + by) for i in range(LAYERS) if 0 <= i + by < LAYERS]
    return lax.ppermute(block, "layer", pairs)


def swap(block):
    return lax.ppermute(block, "c", [(0, 1), (1, 0)])


def of_cores(rows):
    return lax.all_gather(rows, "c", axis=0, tiled=True)


def of_pair(rows):
    return lax.all_gather(rows, "near", axis=0, tiled=True)


def dot(a, b):
    return jnp.dot(a, b, preferred_element_type=jnp.float32)


def dot_across(a, b):
    return lax.dot_general(a, b, (((1,), (1,)), ((), ())), preferred_element_type=jnp.float32)


def inverse(diag):
    order = diag.shape[0]
    eye = jnp.eye(order, dtype=jnp.bool_)
    wide = diag.astype(jnp.float32)
    picked = jnp.where(eye, wide, 0.0)
    across = 1.0 / jnp.sum(picked, axis=0, keepdims=True)
    down = 1.0 / jnp.sum(picked, axis=1, keepdims=True)
    guess = jnp.where(eye, 2.0 * down, 0.0) - down * wide * across
    guess = guess.astype(jnp.bfloat16)
    product = dot(guess, diag).astype(jnp.bfloat16)
    return (2.0 * guess.astype(jnp.float32) - dot(product, guess)).astype(jnp.bfloat16)


def solve_kernel(diag_ref, *refs):
    solved_ref = refs[-1]
    found = inverse(diag_ref[...])
    at = 0
    for ref in refs[:-1]:
        rows = ref.shape[0]
        solved_ref[at : at + rows] = dot(ref[...], found).astype(jnp.bfloat16)
        at += rows


def solve(diag, parts):
    m = diag.shape[0]
    rows = sum(p.shape[0] for p in parts)
    whole = pl.BlockSpec(memory_space=pltpu.VMEM)
    return pl.pallas_call(
        solve_kernel,
        out_shape=jax.ShapeDtypeStruct((rows, m), jnp.bfloat16),
        in_specs=[whole] * (1 + len(parts)),
        out_specs=whole,
        compiler_params=pltpu.CompilerParams(vmem_limit_bytes=24 * 2**20),
        cost_estimate=pl.CostEstimate(flops=2 * m * m * (2 * m + rows), bytes_accessed=4 * m * (m + rows), transcendentals=0),
    )(diag, *parts)


def finish_kernel(core_ref, done_ref, diag_ref, rhs_ref):
    n = diag_ref.shape[1]
    q, g = diag_ref.shape[2] // 4, rhs_ref.shape[2] // 4
    for own in range(2):

        @pl.when(core_ref[0] == own)
        def _(own=own):
            for k in range(4):
                turned = done_ref[k // 2, k % 2].astype(jnp.float32).T
                turned = turned[own * n : own * n + n].astype(jnp.bfloat16)
                diag_ref[0, :, k * q : k * q + q] = turned[:, :q]
                rhs_ref[0, :, k * g : k * g + g] = turned[:, q:]


def finish(done, core, n, m, r):
    whole = pl.BlockSpec(memory_space=pltpu.VMEM)
    shapes = ((1, n, m), (1, n, r))
    return pl.pallas_call(
        finish_kernel,
        out_shape=tuple(jax.ShapeDtypeStruct(s, jnp.bfloat16) for s in shapes),
        in_specs=[pl.BlockSpec(memory_space=pltpu.SMEM), whole],
        out_specs=(whole, whole),
        compiler_params=pltpu.CompilerParams(vmem_limit_bytes=8 * 2**20),
        cost_estimate=pl.CostEstimate(flops=m * n, bytes_accessed=4 * m * n, transcendentals=0),
    )(core.reshape(1).astype(jnp.int32), done)


def after(diag, rhs, left, right):
    h, f = diag.shape[0], rhs.shape[0]
    new_diag = diag.astype(jnp.float32) - left[h + f :] - right[:h]
    new_rhs = rhs.astype(jnp.float32) - left[h : h + f] - right[h : h + f]
    new = (new_diag, -left[:h], -right[h + f :], new_rhs)
    return tuple(a.astype(jnp.bfloat16) for a in new)


def first_kernel(core_ref, mine_ref, other_ref, solved_ref, lower_ref, upper_ref, diag_out, rhs_out, diag_ref, rhs_ref):
    m = diag_ref.shape[0]
    n = mine_ref.shape[1]
    wholes = ((diag_ref, 0, m), (lower_ref, m, m), (upper_ref, 2 * m, m), (rhs_ref, 3 * m, rhs_ref.shape[1]))
    for own in range(2):

        @pl.when(core_ref[0] == own)
        def _(own=own):
            for k in range(mine_ref.shape[0]):
                for ref, c in ((mine_ref, own), (other_ref, 1 - own)):
                    at = (2 * k + c) * n
                    for whole, left, width in wholes:
                        whole[at : at + n] = ref[k, :, left : left + width]

    found = inverse(diag_ref[...])
    q, g = solved_ref.shape[1] // 4, rhs_out.shape[0]
    for k in range(4):

        @pl.when(core_ref[1] == k)
        def _(k=k):
            side = slice(k * q, k * q + q)
            small = slice(k * g, k * g + g)

            def solved(right):
                return dot(found, right).T.astype(jnp.bfloat16)

            solved_ref[:q] = solved(lower_ref[:, side])
            solved_ref[q + g :] = solved(upper_ref[:, side])
            solved_ref[q : q + g] = solved(rhs_ref[:, small])
            diag_out[...] = diag_ref[:, side].T
            rhs_out[...] = rhs_ref[:, small].T


def first_solve(rows, core, quarter, m):
    copies = jnp.broadcast_to(rows[None], (8, *rows.shape))
    mine = lax.all_to_all(copies, ("far", "near"), 0, 0, tiled=True)
    r = rows.shape[1] - 3 * m
    whole = pl.BlockSpec(memory_space=pltpu.VMEM)
    shapes = (((2 * m + r) // 4, m), (m, m), (m, m), (m // 4, m), (r // 4, m))
    return pl.pallas_call(
        first_kernel,
        out_shape=tuple(jax.ShapeDtypeStruct(s, jnp.bfloat16) for s in shapes),
        in_specs=[pl.BlockSpec(memory_space=pltpu.SMEM), whole, whole],
        out_specs=(whole,) * 5,
        scratch_shapes=[pltpu.VMEM((m, m), jnp.bfloat16), pltpu.VMEM((m, r), jnp.bfloat16)],
        compiler_params=pltpu.CompilerParams(vmem_limit_bytes=24 * 2**20),
        cost_estimate=pl.CostEstimate(flops=7 * m * m * m, bytes_accessed=16 * m * m, transcendentals=0),
    )(jnp.stack([core, quarter]).astype(jnp.int32), mine, swap(mine))


def on_device(lower_blocks, diag_blocks, upper_blocks, right_sides):
    core, near = lax.axis_index("c"), lax.axis_index("near")
    m, r = lower_blocks.shape[2], right_sides.shape[2]
    q, g = m // 4, r // 4
    own = (diag_blocks[0], lower_blocks[0], upper_blocks[0], right_sides[0])
    rows = jnp.concatenate(own, axis=1)
    solved, lower, upper, diag, rhs = first_solve(rows, core, core * 2 + near, m)
    left, right = dot_across(send(solved, 1), lower), dot_across(send(solved, -1), upper)
    diag, lower, upper, rhs = after(diag, rhs, left, right)

    solved = solve(of_cores(of_pair(diag)), (lower, rhs, upper))
    solved, lower, upper = lax.optimization_barrier((solved, lower, upper))
    ahead, behind = send(solved, 2), send(solved, -2)
    both = lax.all_gather(jnp.concatenate([lower, upper], axis=0), "near", axis=0)
    lower = of_cores(jnp.concatenate([both[0, :q], both[1, :q]], axis=0))
    upper = of_cores(jnp.concatenate([both[0, q:], both[1, q:]], axis=0))
    diag, lower, upper, rhs = after(diag, rhs, dot(ahead, lower), dot(behind, upper))

    n = own[0].shape[0]
    at = lax.axis_index("far") * (4 * n)

    def rows_of(block):
        return lax.dynamic_slice_in_dim(block, at, 4 * n, axis=1)

    wide = of_pair(jnp.concatenate([diag, rows_of(lower), rows_of(upper)], axis=1))
    solved = solve(of_cores(wide[:, :m]), (lower, rhs, upper))
    solved, couplings = lax.optimization_barrier((solved, wide[:, m:]))
    forward, back = send(solved[q:], 4), send(solved[: q + g], -4)
    couplings = of_cores(couplings)
    left = dot(forward, couplings[:, : 4 * n])
    right = dot(back, couplings[:, 4 * n :])
    new_diag = rows_of(diag).astype(jnp.float32) - left[g:] - right[:q]
    new_rhs = rows_of(rhs).astype(jnp.float32) - left[:g] - right[q:]
    done = jnp.concatenate([new_diag, new_rhs], axis=0).astype(jnp.bfloat16)
    done = lax.all_gather(done, "near", axis=0)
    done = jnp.where(near == 0, done[:, :, : 2 * n], done[:, :, 2 * n :])
    done = lax.all_gather(done, "c", axis=0)
    return finish(done, core, n, m, r)


def solution(mesh):
    finer = Mesh(mesh.devices.reshape(LAYERS, 4, 2, 2), AXES)
    placed = P("layer", ("far", "near", "c"), None)
    return jax.shard_map(
        on_device,
        mesh=finer,
        in_specs=(placed,) * 4,
        out_specs=(placed,) * 2,
        check_vma=False,
    )
```

```python
import jax
import jax.numpy as jnp
from jax import lax
from jax.experimental import pallas as pl
from jax.experimental.pallas import tpu as pltpu
from jax.sharding import Mesh
from jax.sharding import PartitionSpec as P

LAYERS = 32
AXES = ("layer", "far", "near", "c")


def send(block, by):
    pairs = [(i, i + by) for i in range(LAYERS) if 0 <= i + by < LAYERS]
    return lax.ppermute(block, "layer", pairs)


def swap(block):
    return lax.ppermute(block, "c", [(0, 1), (1, 0)])


def of_cores(rows):
    return lax.all_gather(rows, "c", axis=0, tiled=True)


def of_pair(rows):
    return lax.all_gather(rows, "near", axis=0, tiled=True)


def dot(a, b):
    return jnp.dot(a, b, preferred_element_type=jnp.float32)


def dot_across(a, b):
    return lax.dot_general(a, b, (((1,), (1,)), ((), ())), preferred_element_type=jnp.float32)


def inverse(diag):
    order = diag.shape[0]
    eye = jnp.eye(order, dtype=jnp.bool_)
    wide = diag.astype(jnp.float32)
    picked = jnp.where(eye, wide, 0.0)
    across = 1.0 / jnp.sum(picked, axis=0, keepdims=True)
    down = 1.0 / jnp.sum(picked, axis=1, keepdims=True)
    guess = jnp.where(eye, 2.0 * down, 0.0) - down * wide * across
    guess = guess.astype(jnp.bfloat16)
    product = dot(guess, diag).astype(jnp.bfloat16)
    return (2.0 * guess.astype(jnp.float32) - dot(product, guess)).astype(jnp.bfloat16)


def solve_kernel(diag_ref, *refs):
    solved_ref = refs[-1]
    found = inverse(diag_ref[...])
    at = 0
    for ref in refs[:-1]:
        rows = ref.shape[0]
        solved_ref[at : at + rows] = dot(ref[...], found).astype(jnp.bfloat16)
        at += rows


def solve(diag, parts):
    m = diag.shape[0]
    rows = sum(p.shape[0] for p in parts)
    whole = pl.BlockSpec(memory_space=pltpu.VMEM)
    return pl.pallas_call(
        solve_kernel,
        out_shape=jax.ShapeDtypeStruct((rows, m), jnp.bfloat16),
        in_specs=[whole] * (1 + len(parts)),
        out_specs=whole,
        compiler_params=pltpu.CompilerParams(vmem_limit_bytes=24 * 2**20),
        cost_estimate=pl.CostEstimate(flops=2 * m * m * (2 * m + rows), bytes_accessed=4 * m * (m + rows), transcendentals=0),
    )(diag, *parts)


def finish_kernel(core_ref, done_ref, diag_ref, rhs_ref):
    n = diag_ref.shape[1]
    q, g = diag_ref.shape[2] // 4, rhs_ref.shape[2] // 4
    for own in range(2):

        @pl.when(core_ref[0] == own)
        def _(own=own):
            for k in range(4):
                turned = done_ref[k % 2, k // 2].astype(jnp.float32).T
                turned = turned[own * n : own * n + n].astype(jnp.bfloat16)
                diag_ref[0, :, k * q : k * q + q] = turned[:, :q]
                rhs_ref[0, :, k * g : k * g + g] = turned[:, q:]


def finish(done, core, n, m, r):
    whole = pl.BlockSpec(memory_space=pltpu.VMEM)
    shapes = ((1, n, m), (1, n, r))
    return pl.pallas_call(
        finish_kernel,
        out_shape=tuple(jax.ShapeDtypeStruct(s, jnp.bfloat16) for s in shapes),
        in_specs=[pl.BlockSpec(memory_space=pltpu.SMEM), whole],
        out_specs=(whole, whole),
        compiler_params=pltpu.CompilerParams(vmem_limit_bytes=8 * 2**20),
        cost_estimate=pl.CostEstimate(flops=m * n, bytes_accessed=4 * m * n, transcendentals=0),
    )(core.reshape(1).astype(jnp.int32), done)


def after(diag, rhs, left, right):
    h, f = diag.shape[0], rhs.shape[0]
    new_diag = diag.astype(jnp.float32) - left[h + f :] - right[:h]
    new_rhs = rhs.astype(jnp.float32) - left[h : h + f] - right[h : h + f]
    new = (new_diag, -left[:h], -right[h + f :], new_rhs)
    return tuple(a.astype(jnp.bfloat16) for a in new)


def first_kernel(core_ref, mine_ref, other_ref, solved_ref, lower_ref, upper_ref, diag_out, rhs_out, diag_ref, rhs_ref):
    m = diag_ref.shape[0]
    n = mine_ref.shape[1]
    wholes = ((diag_ref, 0, m), (lower_ref, m, m), (upper_ref, 2 * m, m), (rhs_ref, 3 * m, rhs_ref.shape[1]))
    for own in range(2):

        @pl.when(core_ref[0] == own)
        def _(own=own):
            for k in range(mine_ref.shape[0]):
                for ref, c in ((mine_ref, own), (other_ref, 1 - own)):
                    at = (2 * k + c) * n
                    for whole, left, width in wholes:
                        whole[at : at + n] = ref[k, :, left : left + width]

    found = inverse(diag_ref[...])
    q, g = solved_ref.shape[1] // 4, rhs_out.shape[0]
    for k in range(4):

        @pl.when(core_ref[1] == k)
        def _(k=k):
            side = slice(k * q, k * q + q)
            small = slice(k * g, k * g + g)

            def solved(right):
                return dot(found, right).T.astype(jnp.bfloat16)

            solved_ref[:q] = solved(lower_ref[:, side])
            solved_ref[q + g :] = solved(upper_ref[:, side])
            solved_ref[q : q + g] = solved(rhs_ref[:, small])
            diag_out[...] = diag_ref[:, side].T
            rhs_out[...] = rhs_ref[:, small].T


def first_solve(rows, core, quarter, m):
    copies = jnp.broadcast_to(rows[None], (8, *rows.shape))
    mine = lax.all_to_all(copies, ("far", "near"), 0, 0, tiled=True)
    r = rows.shape[1] - 3 * m
    whole = pl.BlockSpec(memory_space=pltpu.VMEM)
    shapes = (((2 * m + r) // 4, m), (m, m), (m, m), (m // 4, m), (r // 4, m))
    return pl.pallas_call(
        first_kernel,
        out_shape=tuple(jax.ShapeDtypeStruct(s, jnp.bfloat16) for s in shapes),
        in_specs=[pl.BlockSpec(memory_space=pltpu.SMEM), whole, whole],
        out_specs=(whole,) * 5,
        scratch_shapes=[pltpu.VMEM((m, m), jnp.bfloat16), pltpu.VMEM((m, r), jnp.bfloat16)],
        compiler_params=pltpu.CompilerParams(vmem_limit_bytes=24 * 2**20),
        cost_estimate=pl.CostEstimate(flops=7 * m * m * m, bytes_accessed=16 * m * m, transcendentals=0),
    )(jnp.stack([core, quarter]).astype(jnp.int32), mine, swap(mine))


def on_device(lower_blocks, diag_blocks, upper_blocks, right_sides):
    core, near = lax.axis_index("c"), lax.axis_index("near")
    m, r = lower_blocks.shape[2], right_sides.shape[2]
    q, g = m // 4, r // 4
    own = (diag_blocks[0], lower_blocks[0], upper_blocks[0], right_sides[0])
    rows = jnp.concatenate(own, axis=1)
    solved, lower, upper, diag, rhs = first_solve(rows, core, core * 2 + near, m)
    left, right = dot_across(send(solved, 1), lower), dot_across(send(solved, -1), upper)
    diag, lower, upper, rhs = after(diag, rhs, left, right)

    solved = solve(of_cores(of_pair(diag)), (lower, rhs, upper))
    solved, lower, upper = lax.optimization_barrier((solved, lower, upper))
    ahead, behind = send(solved, 2), send(solved, -2)
    both = lax.all_gather(jnp.concatenate([lower, upper], axis=0), "near", axis=0)
    lower = of_cores(jnp.concatenate([both[0, :q], both[1, :q]], axis=0))
    upper = of_cores(jnp.concatenate([both[0, q:], both[1, q:]], axis=0))
    diag, lower, upper, rhs = after(diag, rhs, dot(ahead, lower), dot(behind, upper))

    n = own[0].shape[0]
    at = lax.axis_index("far") * (4 * n)

    def rows_of(block):
        return lax.dynamic_slice_in_dim(block, at, 4 * n, axis=1)

    wide = of_pair(jnp.concatenate([diag, rows_of(lower), rows_of(upper)], axis=1))
    solved = solve(of_cores(wide[:, :m]), (lower, rhs, upper))
    solved, couplings = lax.optimization_barrier((solved, wide[:, m:]))
    forward, back = send(solved[q:], 4), send(solved[: q + g], -4)
    couplings = of_cores(couplings)
    left = dot(forward, couplings[:, : 4 * n])
    right = dot(back, couplings[:, 4 * n :])
    new_diag = rows_of(diag).astype(jnp.float32) - left[g:] - right[:q]
    new_rhs = rows_of(rhs).astype(jnp.float32) - left[:g] - right[q:]
    done = jnp.concatenate([new_diag, new_rhs], axis=0).astype(jnp.bfloat16)
    done = lax.all_gather(done, "c", axis=0)
    low = jnp.concatenate([done[..., :n], done[..., 2 * n : 3 * n]], axis=-1)
    high = jnp.concatenate([done[..., n : 2 * n], done[..., 3 * n :]], axis=-1)
    done = lax.all_gather(jnp.where(core == 0, low, high), "near", axis=0)
    return finish(done, near, n, m, r)


def solution(mesh):
    finer = Mesh(mesh.devices.reshape(LAYERS, 4, 2, 2), AXES)
    placed = P("layer", ("far", "near", "c"), None)
    return jax.shard_map(
        on_device,
        mesh=finer,
        in_specs=(placed,) * 4,
        out_specs=(placed,) * 2,
        check_vma=False,
    )
```
